512 devices in a mesh: ta: 128 (over y_hi, x, z), gz: 4 (over y_lo, core).
Axes of the slice: x: 4, y: 8 (y_hi: 4, y_lo: 2; y = y_hi * 2 + y_lo), z: 8, core: 2. Of those that a mesh axis runs over, the one named last changes fastest.
Arguments:
- source: bfloat16 [128, 8, 4, 4, 64, 128], P('ta', 'gz'), may hold values from -6 to 6
- self_codes: bfloat16 [128, 8, 4, 4, 64, 64], P('ta', 'gz'), may hold values from -6 to 6
- hop_codes: bfloat16 [128, 8, 4, 4, 64, 256], P('ta', 'gz'), may hold values from -6 to 6
- link_scales: bfloat16 [128, 8, 4, 4, 5], P('ta', 'gz'), may hold values from 0.019897461 to 0.079589844
- restrict_map: int32 [128, 8, 4, 4], P('ta', 'gz'), may hold values from 0 to 15
- restrictor: bfloat16 [128, 8, 4, 4, 64, 64], P('ta', 'gz'), may hold values from -0.75 to 0.75
Outputs:
- smoothed: bfloat16 [128, 8, 4, 4, 64, 128], P('ta', 'gz')
- coarse: float32 [128, 16, 64, 128], P('ta', 'gz')
The draws below stay inside these ranges and needn't reach their ends.
All inputs are finite; a program needn't handle non-finite values.
Results may differ from the reference program's by a relative error of at most 0.0041.
Values may be sent and summed in bfloat16 or wider, within the bound.
No kernel may reach another device: no remote copies, remote signals or barrier semaphores. Data moves between devices by JAX's collectives and lax.ppermute only.
A program may use at most 64 MiB of HBM per device.

```python
import math
import jax
import jax.numpy as jnp
from jax import lax

NV = 64
NVC = 64
RHS = 128
T_DEV = 1
XS = 4
YS = 4
ITERS = 3
TT = 128
ZZ = 8
AGG = 16


def plant(values, own_key, low, top_value):
    index_at = [jax.random.randint(jax.random.fold_in(own_key, axis), (), 0, length) for axis, length in enumerate(values.shape)]
    longest = values.shape.index(max(values.shape))
    next_to = index_at[:longest] + [(index_at[longest] + 1) % values.shape[longest]] + index_at[longest + 1:]
    return values.at[tuple(index_at)].set(low).at[tuple(next_to)].set(top_value)


def levels(stream_key, dims, pieces, least, high):
    loudness = 1.0
    for position, blocks in pieces:
        draws = jax.random.uniform(jax.random.fold_in(jax.random.fold_in(stream_key, 6), position), (blocks,), jnp.float32, least / len(pieces), high / len(pieces))
        loudness = loudness * jnp.repeat(jnp.exp(draws), dims[position] // blocks).reshape((-1,) + (1,) * (len(dims) - 1 - position))
    return loudness


def scatter_about(own_key, shape, scale, limit, pieces=(), kind=jnp.bfloat16):
    factor_of = levels(own_key, shape, pieces, -0.22, 0.18) if pieces else 1.0
    values = jax.random.normal(own_key, shape, jnp.float32) * scale * factor_of
    return jnp.minimum(jnp.maximum(values, -limit), limit).astype(kind)


def setup_inputs(seed: int = 0) -> dict:
    keys = jax.random.split(jax.random.key(seed), 7)
    source = scatter_about(keys[0], (TT, ZZ, XS, YS, NV, RHS), 1.0, 6.0, ((0, 128), (1, 4)))
    self_codes = scatter_about(keys[1], (TT, ZZ, XS, YS, NV, NV), 1.0, 6.0, ((0, 128), (1, 4)))
    hop_codes = scatter_about(keys[2], (TT, ZZ, XS, YS, NV, 4 * NV), 1.0, 6.0, ((0, 128), (1, 4)))
    link_scales = jnp.clip(jnp.exp(math.log(0.079589844) - 1.3862944 * jax.random.uniform(keys[3], (TT, ZZ, XS, YS, 5), jnp.float32) ** levels(keys[3], (TT, ZZ, XS, YS, 5), ((0, 128), (1, 4)), -0.2, 0.2)), 0.019897461, 0.079589844).astype(jnp.bfloat16)
    restrict_map = plant(jax.random.randint(keys[4], (TT, ZZ, XS, YS), 0, AGG), jax.random.fold_in(keys[4], 1), 0, AGG - 1).astype(jnp.int32)
    restrictor = scatter_about(keys[5], (TT, ZZ, XS, YS, NVC, NV), NV ** -0.5, 0.75, ((0, 128), (1, 4)))
    return dict(source=source, self_codes=self_codes, hop_codes=hop_codes, link_scales=link_scales, restrict_map=restrict_map, restrictor=restrictor)


OMEGA = 0.5


def slice_mult(codes, vector):
    return jnp.einsum('zxyab,zxybr->zxyar', codes.astype(jnp.float32), vector.astype(jnp.float32))


def slice_mult_transposed(codes, vector):
    return jnp.einsum('zxyab,zxyar->zxybr', codes.astype(jnp.float32), vector.astype(jnp.float32))


def block_of(hops, direction):
    degrees = hops.shape[-2]
    return hops[..., direction * degrees:(direction + 1) * degrees]


def operate_on(vector_field, self_codes, hop_codes, link_scales):
    extent = vector_field.shape[0]

    def one_slice(slice_index):
        after = (slice_index + 1) % extent
        before = (slice_index - 1 + extent) % extent
        center = vector_field[slice_index]
        ahead_field = vector_field[after]
        prior_field = vector_field[before]
        scales = link_scales[slice_index].astype(jnp.float32)
        hops = hop_codes[slice_index]
        result = center.astype(jnp.float32) + scales[..., 0][..., None, None] * slice_mult(self_codes[slice_index], center)
        neighbours = [jnp.roll(center, -1, 1), jnp.roll(center, -1, 2), jnp.roll(center, -1, 0), ahead_field]
        roll_axes = [1, 2, 0]
        for direction in range(4):
            link_block = block_of(hops, direction)
            factor = scales[..., direction + 1][..., None, None]
            result = result + factor * slice_mult(link_block, neighbours[direction])
            if direction < 3:
                behind_term = (factor * slice_mult_transposed(link_block, center)).astype(jnp.bfloat16)
                shifted = jnp.roll(behind_term, 1, axis=roll_axes[direction])
            else:
                prior_factor = link_scales[before][..., 4].astype(jnp.float32)[..., None, None]
                prior_block = block_of(hop_codes[before], 3)
                shifted = (prior_factor * slice_mult_transposed(prior_block, prior_field)).astype(jnp.bfloat16)
            result = result + shifted.astype(jnp.float32)
        return result

    return lax.map(one_slice, jnp.arange(extent, dtype=jnp.int32))


def reference(source, self_codes, hop_codes, link_scales, restrict_map, restrictor):
    source_float = source.astype(jnp.float32)
    estimate = source_float
    vector_field = source
    for iteration in range(ITERS):
        applied = operate_on(vector_field, self_codes, hop_codes, link_scales)
        estimate = estimate + OMEGA * (source_float - applied)
        vector_field = estimate.astype(jnp.bfloat16)
    smoothed = vector_field
    columns = smoothed.shape[0] // T_DEV

    def one_column(column):
        start = (column * T_DEV).astype(jnp.int32)
        slab_rows = lax.dynamic_slice_in_dim(smoothed, start, T_DEV, 0)
        slab_restrict = lax.dynamic_slice_in_dim(restrictor, start, T_DEV, 0)
        labels = lax.dynamic_slice_in_dim(restrict_map, start, T_DEV, 0).reshape(-1)
        projected = jnp.einsum('tzxyca,tzxyar->tzxycr', slab_restrict.astype(jnp.float32), slab_rows.astype(jnp.float32))
        flattened = projected.reshape(labels.shape[0], NVC * RHS)
        onehot = (labels[None, :] == jnp.arange(AGG, dtype=jnp.int32)[:, None]).astype(jnp.float32)
        summed = jnp.dot(onehot, flattened, precision=lax.Precision.HIGHEST)
        return summed.reshape(AGG, NVC, RHS)

    coarse = lax.map(one_column, jnp.arange(columns, dtype=jnp.int32))
    return smoothed, coarse
```

```python
import functools

import jax
import jax.numpy as jnp
from jax import lax
from jax.experimental import pallas as pl
from jax.experimental.pallas import tpu as pltpu
from jax.sharding import PartitionSpec as P

ITERS = 3
OMEGA = 0.5
F32 = jnp.float32
BF16 = jnp.bfloat16
VMEM = pl.BlockSpec(memory_space=pltpu.VMEM)
SMEM = pl.BlockSpec(memory_space=pltpu.SMEM)
PARAMS = pltpu.CompilerParams(vmem_limit_bytes=12 * 1024 * 1024)


def shifted(block, axis, distance):
    n = lax.axis_size(axis)
    return lax.ppermute(block, axis, [((i - distance) % n, i) for i in range(n)])


def dot(a, b):
    return jnp.dot(a, b, preferred_element_type=F32)


def dot_t(a, b):
    return lax.dot_general(a, b, (((0,), (0,)), ((), ())), preferred_element_type=F32)


def first_terms(scales, vector, hops, t_terms, z_terms):
    sites, degrees = vector.shape[:2]
    last = sites - z_terms.shape[0]
    for s in range(sites):
        p = vector[s]
        t_terms[s] = (scales[5 * s + 4] * dot_t(hops[s, :, 3 * degrees :], p)).astype(BF16)
        if s >= last:
            z_terms[s - last] = (scales[5 * s + 3] * dot_t(hops[s, :, 2 * degrees : 3 * degrees], p)).astype(BF16)


def local_terms(shape, scales, estimate, source, vector, selfs, hops, z_next, z_back, partial):
    zs, xs, ys, d = shape

    def at(z, x, y):
        return (z * xs + x % xs) * ys + y % ys

    def fwd(m, s, p):
        return scales[5 * s + m + 1] * dot(hops[s, :, m * d : (m + 1) * d], p)

    def bwd(m, s):
        return scales[5 * s + m + 1] * dot_t(hops[s, :, m * d : (m + 1) * d], vector[s])

    for z in range(zs):
        for x in range(xs):
            for y in range(ys):
                s = at(z, x, y)
                p = vector[s]
                total = p.astype(F32) + scales[5 * s] * dot(selfs[s], p)
                total += fwd(0, s, vector[at(z, x + 1, y)])
                total += fwd(1, s, vector[at(z, x, y + 1)])
                total += fwd(2, s, vector[at(z + 1, x, y)] if z + 1 < zs else z_next[at(0, x, y)])
                total += bwd(0, at(z, x - 1, y))
                total += bwd(1, at(z, x, y - 1))
                total += bwd(2, at(z - 1, x, y)) if z else z_back[at(0, x, y)].astype(F32)
                partial[s] = estimate[s].astype(F32) + OMEGA * (source[s].astype(F32) - total)


def finish(sites, scales, partial, t_next, t_back, hops, s, d):
    total = scales[5 * s + 4] * dot(hops[s, :, 3 * d :], t_next[s]) + t_back[s].astype(F32)
    return partial[s] - OMEGA * total


def sweep_end(scales, partial, t_next, t_back, hops, estimate, vector, t_terms, z_terms):
    sites, d = vector.shape[:2]
    last = sites - z_terms.shape[0]
    for s in range(sites):
        e = finish(sites, scales, partial, t_next, t_back, hops, s, d)
        p = e.astype(BF16)
        estimate[s] = e
        vector[s] = p
        t_terms[s] = (scales[5 * s + 4] * dot_t(hops[s, :, 3 * d :], p)).astype(BF16)
        if s >= last:
            z_terms[s - last] = (scales[5 * s + 3] * dot_t(hops[s, :, 2 * d : 3 * d], p)).astype(BF16)


def last_end(peers, scales, labels, place, partial, t_next, t_back, hops, restrictor, vector, own, *rest):
    away, sums = rest[:-1], rest[-1]
    sites, d = vector.shape[:2]
    keep = own.shape[0]
    sums[...] = jnp.zeros_like(sums)
    for s in range(sites):
        p = finish(sites, scales, partial, t_next, t_back, hops, s, d).astype(BF16)
        vector[s] = p
        sums[labels[s]] += dot(restrictor[s], p)
    me = place[0]
    own[...] = sums[pl.ds(me * keep, keep)]
    for j, out in enumerate(away, 1):
        out[...] = sums[pl.ds((me ^ j) * keep, keep)].astype(BF16)


def shards(source, self_codes, hop_codes, link_scales, restrict_map, restrictor):
    ts, zs, xs, ys, d, cols = source.shape
    assert ts == 1
    sites, edge = zs * xs * ys, xs * ys
    b = source.reshape(sites, d, cols)
    selfs = self_codes.reshape(sites, d, d)
    hops = hop_codes.reshape(sites, d, 4 * d)
    restricts = restrictor.reshape(sites, -1, d)
    scales = link_scales.astype(F32).reshape(sites * 5)
    labels = restrict_map.reshape(sites)
    field = jax.ShapeDtypeStruct((sites, d, cols), BF16)
    wide = jax.ShapeDtypeStruct((sites, d, cols), F32)
    slab = jax.ShapeDtypeStruct((edge, d, cols), BF16)

    t_terms, z_terms = pl.pallas_call(
        first_terms,
        out_shape=(field, slab),
        in_specs=[SMEM, VMEM, VMEM],
        out_specs=(VMEM, VMEM),
        compiler_params=PARAMS,
    )(scales, b, hops)
    vector, estimate = b, b
    for sweep in range(ITERS):
        t_back = shifted(t_terms, "ta", 1)
        t_next = shifted(vector, "ta", -1)
        z_next = shifted(vector[:edge], "gz", -1)
        z_back = shifted(z_terms, "gz", 1)
        partial = pl.pallas_call(
            functools.partial(local_terms, (zs, xs, ys, d)),
            out_shape=wide,
            in_specs=[SMEM] + [VMEM] * 7,
            out_specs=VMEM,
            compiler_params=PARAMS,
        )(scales, estimate, b, vector, selfs, hops, z_next, z_back)
        if sweep + 1 < ITERS:
            estimate, vector, t_terms, z_terms = pl.pallas_call(
                sweep_end,
                out_shape=(wide, field, field, slab),
                in_specs=[SMEM] + [VMEM] * 3 + [VMEM],
                out_specs=(VMEM,) * 4,
                compiler_params=PARAMS,
            )(scales, partial, t_next, t_back, hops)
    peers = lax.axis_size("gz")
    keep = 16 // peers
    coarse_d = restricts.shape[1]
    own_shape = jax.ShapeDtypeStruct((keep, coarse_d, cols), F32)
    away_shape = jax.ShapeDtypeStruct((keep, coarse_d, cols), BF16)
    place = lax.axis_index("gz").reshape(1).astype(jnp.int32)
    smoothed, own, *away = pl.pallas_call(
        functools.partial(last_end, peers),
        out_shape=(field, own_shape) + (away_shape,) * (peers - 1),
        in_specs=[SMEM] * 3 + [VMEM] * 3 + [VMEM, VMEM],
        out_specs=(VMEM,) * (peers + 1),
        scratch_shapes=[pltpu.VMEM((keep * peers, coarse_d, cols), F32)],
        compiler_params=PARAMS,
    )(scales, labels, place, partial, t_next, t_back, hops, restricts)
    came = [
        lax.ppermute(part, "gz", [(i, i ^ j) for i in range(peers)]) for j, part in enumerate(away, 1)
    ]
    coarse = own
    for part in came:
        coarse = coarse + part.astype(F32)
    return smoothed.reshape(source.shape), coarse.reshape(1, keep, coarse_d, cols)


def solution(mesh):
    site = P("ta", "gz", None, None, None, None)
    return jax.shard_map(
        shards,
        mesh=mesh,
        in_specs=(site, site, site, P("ta", "gz", None, None, None), P("ta", "gz", None, None), site),
        out_specs=(site, P("ta", "gz", None, None)),
        check_vma=False,
    )
```

```python
import functools

import jax
import jax.numpy as jnp
from jax import lax
from jax.experimental import pallas as pl
from jax.experimental.pallas import tpu as pltpu
from jax.sharding import PartitionSpec as P

ITERS = 3
OMEGA = 0.5
AGG = 16
PIECES = 4
F32 = jnp.float32
BF16 = jnp.bfloat16
VMEM = pl.BlockSpec(memory_space=pltpu.VMEM)
HBM = pl.BlockSpec(memory_space=pltpu.HBM)
SMEM = pl.BlockSpec(memory_space=pltpu.SMEM)
PARAMS = pltpu.CompilerParams(vmem_limit_bytes=12 * 1024 * 1024)

GROUP = 32
FORWARD_RELAY = {1: 24, 2: 0, 3: 7}
BACKWARD_RELAY = {1: 7, 2: 31, 3: 24}
FORWARD_SEAM, BACKWARD_SEAM = 1, 2


def routes(slices, members):
    forward, backward, out, back = [], [], [], []
    for t in range(slices):
        for g in range(members):
            here, ahead, behind = (((t + k) % slices) * members + g for k in (0, 1, -1))
            first = t // GROUP * GROUP
            if t % GROUP == GROUP - 1 and g in FORWARD_RELAY:
                relay = (first + FORWARD_RELAY[g]) * members + g
                out.append((here, relay))
                back.append((relay, ahead))
            else:
                forward.append((here, ahead))
            if t % GROUP == 0 and g in BACKWARD_RELAY:
                relay = (first + BACKWARD_RELAY[g]) * members + g
                out.append((here, relay))
                back.append((relay, behind))
            else:
                backward.append((here, behind))
    return forward, backward, out, back


def shifted(block, axis, distance):
    n = lax.axis_size(axis)
    return lax.ppermute(block, axis, [((i - distance) % n, i) for i in range(n)])


def dot(a, b):
    return jnp.dot(a, b, preferred_element_type=F32)


def dot_t(a, b):
    return lax.dot_general(a, b, (((0,), (0,)), ((), ())), preferred_element_type=F32)


def fill_detour(role, t_terms, vector, detour):
    @pl.when(role[0] == FORWARD_SEAM)
    def _():
        detour[...] = t_terms[...]

    @pl.when(role[0] == BACKWARD_SEAM)
    def _():
        detour[...] = vector[...]


def first_terms(role, scales, source, hops, t_terms, z_terms, detour, vector, codes, sems):
    sites, d = vector.shape[:2]
    xs, ys = scales.shape[2:4]
    last = sites - z_terms.shape[0]
    pieces = sems.shape[1]
    n = sites // pieces
    copies = []
    for i in range(pieces):
        part = pl.ds(i * n, n)
        copies.append(
            [
                pltpu.make_async_copy(hops.at[part, :, pl.ds(2 * d, 2 * d)], codes.at[part], sems.at[0, i]),
                pltpu.make_async_copy(source.at[part], vector.at[part], sems.at[1, i]),
            ]
        )
    for pair in copies:
        for copy in pair:
            copy.start()
    for s in range(sites):
        if s % n == 0:
            for copy in copies[s // n]:
                copy.wait()
        z, x, y = s // (xs * ys), s // ys % xs, s % ys
        scale = scales[0, z, x].astype(F32)
        t_terms[s] = (scale[y : y + 1, 4:5] * dot_t(codes[s, :, d:], vector[s])).astype(BF16)
        if s >= last:
            z_terms[s - last] = (scale[y : y + 1, 3:4] * dot_t(codes[s, :, :d], vector[s])).astype(BF16)
    fill_detour(role, t_terms, vector, detour)


def hop_terms(role, scales, vector, hops, t_terms, z_terms, detour):
    sites, d = vector.shape[:2]
    last = sites - z_terms.shape[0]
    for s in range(sites):
        t_terms[s] = (scales[5 * s + 4] * dot_t(hops[s, :, 3 * d :], vector[s])).astype(BF16)
    for s in range(last, sites):
        z_terms[s - last] = (scales[5 * s + 3] * dot_t(hops[s, :, 2 * d : 3 * d], vector[s])).astype(BF16)
    fill_detour(role, t_terms, vector, detour)


def local_terms(shape, scales, estimate, source, vector, selfs, hops, partial):
    zs, xs, ys, d = shape

    def at(z, x, y):
        return (z * xs + x % xs) * ys + y % ys

    def fwd(m, s, p):
        return scales[5 * s + m + 1] * dot(hops[s, :, m * d : (m + 1) * d], p)

    def bwd(m, s):
        return scales[5 * s + m + 1] * dot_t(hops[s, :, m * d : (m + 1) * d], vector[s])

    for z in range(zs):
        for x in range(xs):
            for y in range(ys):
                s = at(z, x, y)
                p = vector[s]
                total = p.astype(F32) + scales[5 * s] * dot(selfs[s], p)
                total += fwd(0, s, vector[at(z, x + 1, y)])
                total += fwd(1, s, vector[at(z, x, y + 1)])
                total += bwd(0, at(z, x - 1, y))
                total += bwd(1, at(z, x, y - 1))
                if z + 1 < zs:
                    total += fwd(2, s, vector[at(z + 1, x, y)])
                if z:
                    total += bwd(2, at(z - 1, x, y))
                partial[s] = estimate[s].astype(F32) + OMEGA * (source[s].astype(F32) - total)


def new_estimate(s, role, scales, partial, t_next, t_back, relayed, z_next, z_back, hops):
    sites, d = partial.shape[:2]
    edge = z_next.shape[0]
    last = sites - edge
    ahead = jnp.where(role[0] == FORWARD_SEAM, relayed[s], t_next[s])
    behind = jnp.where(role[0] == BACKWARD_SEAM, relayed[s], t_back[s])
    total = scales[5 * s + 4] * dot(hops[s, :, 3 * d :], ahead) + behind.astype(F32)
    if s >= last:
        total += scales[5 * s + 3] * dot(hops[s, :, 2 * d : 3 * d], z_next[s - last])
    if s < edge:
        total += z_back[s].astype(F32)
    return partial[s] - OMEGA * total


def sweep_end(role, scales, partial, t_next, t_back, relayed, z_next, z_back, hops, estimate, vector, *terms):
    for s in range(vector.shape[0]):
        e = new_estimate(s, role, scales, partial, t_next, t_back, relayed, z_next, z_back, hops)
        estimate[s] = e
        vector[s] = e.astype(BF16)
    hop_terms(role, scales, vector, hops, *terms)


def last_end(role, scales, labels, partial, t_next, t_back, relayed, z_next, z_back, hops, restrictor, vector, own, away, sums):
    half = own.shape[0] // 2
    sums[...] = jnp.zeros_like(sums)
    for s in range(vector.shape[0]):
        e = new_estimate(s, role, scales, partial, t_next, t_back, relayed, z_next, z_back, hops)
        vector[s] = e.astype(BF16)
    for s in range(vector.shape[0]):
        sums[labels[s]] += dot(restrictor[s], vector[s])
    core = role[1] % 2
    for chip in range(2):
        rows = pl.ds(chip * half, half)
        own[rows] = sums[pl.ds((2 * chip + core) * half, half)]
        away[rows] = sums[pl.ds((2 * chip + 1 - core) * half, half)].astype(BF16)


def coarse_step(role, own, came, mine, away):
    half = mine.shape[0]
    chip = role[1] // 2
    here, there = pl.ds(chip * half, half), pl.ds((1 - chip) * half, half)
    mine[...] = own[here] + came[here].astype(F32)
    away[...] = (own[there] + came[there].astype(F32)).astype(BF16)


def shards(source, self_codes, hop_codes, link_scales, restrict_map, restrictor):
    ts, zs, xs, ys, d, cols = source.shape
    assert ts == 1
    sites, edge = zs * xs * ys, xs * ys
    slices, members = lax.axis_size("ta"), lax.axis_size("gz")
    forward, backward, out, back = routes(slices, members)
    t, g = lax.axis_index("ta"), lax.axis_index("gz")
    seam = jnp.where(t % GROUP == GROUP - 1, FORWARD_SEAM, jnp.where(t % GROUP == 0, BACKWARD_SEAM, 0))
    role = jnp.stack([jnp.where(g == 0, 0, seam), g]).astype(jnp.int32)

    b = source.reshape(sites, d, cols)
    selfs = self_codes.reshape(sites, d, d)
    hops = hop_codes.reshape(sites, d, 4 * d)
    restricts = restrictor.reshape(sites, -1, d)
    labels = restrict_map.reshape(sites)
    field = jax.ShapeDtypeStruct((sites, d, cols), BF16)
    wide = jax.ShapeDtypeStruct((sites, d, cols), F32)
    slab = jax.ShapeDtypeStruct((edge, d, cols), BF16)
    both = ("ta", "gz")

    t_terms, z_terms, detour = pl.pallas_call(
        first_terms,
        out_shape=(field, slab, field),
        in_specs=[SMEM, VMEM, HBM, HBM],
        out_specs=(VMEM,) * 3,
        scratch_shapes=[
            pltpu.VMEM((sites, d, cols), BF16),
            pltpu.VMEM((sites, d, 2 * d), BF16),
            pltpu.SemaphoreType.DMA((2, PIECES)),
        ],
        compiler_params=PARAMS,
    )(role, link_scales, b, hops)
    late_scales, t_terms = lax.optimization_barrier((link_scales, t_terms))
    scales = late_scales.astype(F32).reshape(sites * 5)
    vector, estimate = b, b
    for sweep in range(ITERS):
        at_relay = lax.ppermute(detour, both, out)
        t_back = lax.ppermute(t_terms, both, forward)
        t_next = lax.ppermute(vector, both, backward)
        z_next = shifted(vector[:edge], "gz", -1)
        z_back = shifted(z_terms, "gz", 1)
        partial = pl.pallas_call(
            functools.partial(local_terms, (zs, xs, ys, d)),
            out_shape=wide,
            in_specs=[SMEM] + [VMEM] * 5,
            out_specs=VMEM,
            input_output_aliases={1: 0} if sweep else {},
            compiler_params=PARAMS,
        )(scales, estimate, b, vector, selfs, hops)
        relayed = lax.ppermute(at_relay, both, back)
        came = (partial, t_next, t_back, relayed, z_next, z_back, hops)
        if sweep + 1 < ITERS:
            estimate, vector, t_terms, z_terms, detour = pl.pallas_call(
                sweep_end,
                out_shape=(wide, field, field, slab, field),
                in_specs=[SMEM] * 2 + [VMEM] * 7,
                out_specs=(VMEM,) * 5,
                input_output_aliases={2: 0},
                compiler_params=PARAMS,
            )(role, scales, *came)
    keep = AGG // members
    coarse_d = restricts.shape[1]
    chunk = (keep, coarse_d, cols)
    pair = (2 * keep, coarse_d, cols)
    smoothed, own, away = pl.pallas_call(
        last_end,
        out_shape=(field, jax.ShapeDtypeStruct(pair, F32), jax.ShapeDtypeStruct(pair, BF16)),
        in_specs=[SMEM] * 3 + [VMEM] * 8,
        out_specs=(VMEM,) * 3,
        scratch_shapes=[pltpu.VMEM((AGG, coarse_d, cols), F32)],
        compiler_params=PARAMS,
    )(role, scales, labels, *came, restricts)
    from_core = lax.ppermute(away, "gz", [(i, i ^ 1) for i in range(members)])
    mine, away = pl.pallas_call(
        coarse_step,
        out_shape=(jax.ShapeDtypeStruct(chunk, F32), jax.ShapeDtypeStruct(chunk, BF16)),
        in_specs=[SMEM] + [VMEM] * 2,
        out_specs=(VMEM,) * 2,
        compiler_params=PARAMS,
    )(role, own, from_core)
    from_chip = lax.ppermute(away, "gz", [(i, i ^ 2) for i in range(members)])
    coarse = mine + from_chip.astype(F32)
    return smoothed.reshape(source.shape), coarse.reshape(1, keep, coarse_d, cols)


def solution(mesh):
    site = P("ta", "gz", None, None, None, None)
    return jax.shard_map(
        shards,
        mesh=mesh,
        in_specs=(site, site, site, P("ta", "gz", None, None, None), P("ta", "gz", None, None), site),
        out_specs=(site, P("ta", "gz", None, None)),
        check_vma=False,
    )
```

```python
import functools

import jax
import jax.numpy as jnp
from jax import lax
from jax.experimental import pallas as pl
from jax.experimental.pallas import tpu as pltpu
from jax.sharding import PartitionSpec as P

ITERS = 3
OMEGA = 0.5
AGG = 16
F32 = jnp.float32
BF16 = jnp.bfloat16
VMEM = pl.BlockSpec(memory_space=pltpu.VMEM)
SMEM = pl.BlockSpec(memory_space=pltpu.SMEM)
PARAMS = pltpu.CompilerParams(vmem_limit_bytes=12 * 1024 * 1024)

GROUP = 32
FORWARD_RELAY = {1: 7, 3: 24}
BACKWARD_RELAY = {1: 24, 3: 7}
FORWARD_SEAM, BACKWARD_SEAM = 1, 2


def routes(slices, members):
    forward, backward, out, back = [], [], [], []
    for t in range(slices):
        for g in range(members):
            here, ahead, behind = (((t + k) % slices) * members + g for k in (0, 1, -1))
            first = t // GROUP * GROUP
            if t % GROUP == GROUP - 1 and g in FORWARD_RELAY:
                relay = (first + FORWARD_RELAY[g]) * members + g
                out.append((here, relay))
                back.append((relay, ahead))
            else:
                forward.append((here, ahead))
            if t % GROUP == 0 and g in BACKWARD_RELAY:
                relay = (first + BACKWARD_RELAY[g]) * members + g
                out.append((here, relay))
                back.append((relay, behind))
            else:
                backward.append((here, behind))
    return forward, backward, out, back


def shifted(block, axis, distance):
    n = lax.axis_size(axis)
    return lax.ppermute(block, axis, [((i - distance) % n, i) for i in range(n)])


def dot(a, b):
    return jnp.dot(a, b, preferred_element_type=F32)


def dot_t(a, b):
    return lax.dot_general(a, b, (((0,), (0,)), ((), ())), preferred_element_type=F32)


def hop_terms(role, scales, vector, hops, t_terms, z_terms, detour):
    sites, d = vector.shape[:2]
    last = sites - z_terms.shape[0]
    for s in range(sites):
        t_terms[s] = (scales[5 * s + 4] * dot_t(hops[s, :, 3 * d :], vector[s])).astype(BF16)
    for s in range(last, sites):
        z_terms[s - last] = (scales[5 * s + 3] * dot_t(hops[s, :, 2 * d : 3 * d], vector[s])).astype(BF16)
    for seam, field in ((FORWARD_SEAM, t_terms), (BACKWARD_SEAM, vector)):

        @pl.when(role[0] == seam)
        def _():
            detour[...] = field[...]


def local_terms(shape, scales, estimate, source, vector, selfs, hops, partial):
    zs, xs, ys, d = shape

    def at(z, x, y):
        return (z * xs + x % xs) * ys + y % ys

    def fwd(m, s, p):
        return scales[5 * s + m + 1] * dot(hops[s, :, m * d : (m + 1) * d], p)

    def bwd(m, s):
        return scales[5 * s + m + 1] * dot_t(hops[s, :, m * d : (m + 1) * d], vector[s])

    for z in range(zs):
        for x in range(xs):
            for y in range(ys):
                s = at(z, x, y)
                p = vector[s]
                total = p.astype(F32) + scales[5 * s] * dot(selfs[s], p)
                total += fwd(0, s, vector[at(z, x + 1, y)])
                total += fwd(1, s, vector[at(z, x, y + 1)])
                total += bwd(0, at(z, x - 1, y))
                total += bwd(1, at(z, x, y - 1))
                if z + 1 < zs:
                    total += fwd(2, s, vector[at(z + 1, x, y)])
                if z:
                    total += bwd(2, at(z - 1, x, y))
                partial[s] = estimate[s].astype(F32) + OMEGA * (source[s].astype(F32) - total)


def z_edge_terms(scales, partial, z_next, z_back, hops, done):
    sites, d = partial.shape[:2]
    edge = z_next.shape[0]
    last = sites - edge
    for s in range(edge):
        done[s] = partial[s] - OMEGA * z_back[s].astype(F32)
    for s in range(last, sites):
        done[s] = partial[s] - OMEGA * scales[5 * s + 3] * dot(hops[s, :, 2 * d : 3 * d], z_next[s - last])


def new_estimate(s, role, scales, partial, t_next, t_back, relayed, hops):
    d = partial.shape[1]
    ahead = jnp.where(role[0] == FORWARD_SEAM, relayed[s], t_next[s])
    behind = jnp.where(role[0] == BACKWARD_SEAM, relayed[s], t_back[s])
    total = scales[5 * s + 4] * dot(hops[s, :, 3 * d :], ahead) + behind.astype(F32)
    return partial[s] - OMEGA * total


def sweep_end(role, scales, partial, t_next, t_back, relayed, hops, estimate, vector, *terms):
    for s in range(vector.shape[0]):
        e = new_estimate(s, role, scales, partial, t_next, t_back, relayed, hops)
        estimate[s] = e
        vector[s] = e.astype(BF16)
    hop_terms(role, scales, vector, hops, *terms)


def last_end(role, scales, labels, partial, t_next, t_back, relayed, hops, restrictor, vector, own, away, sums):
    half = own.shape[0] // 2
    xs, ys = labels.shape[2:]
    sums[...] = jnp.zeros_like(sums)
    for s in range(vector.shape[0]):
        e = new_estimate(s, role, scales, partial, t_next, t_back, relayed, hops)
        vector[s] = e.astype(BF16)
    for s in range(vector.shape[0]):
        label = labels[0, s // (xs * ys), s // ys % xs, s % ys]
        sums[label] += dot(restrictor[s], vector[s])
    core = role[1] % 2
    for chip in range(2):
        rows = pl.ds(chip * half, half)
        own[rows] = sums[pl.ds((2 * chip + core) * half, half)]
        away[rows] = sums[pl.ds((2 * chip + 1 - core) * half, half)].astype(BF16)


def coarse_step(role, own, came, mine, away):
    half = mine.shape[0]
    chip = role[1] // 2
    here, there = pl.ds(chip * half, half), pl.ds((1 - chip) * half, half)
    mine[...] = own[here] + came[here].astype(F32)
    away[...] = (own[there] + came[there].astype(F32)).astype(BF16)


def shards(source, self_codes, hop_codes, link_scales, restrict_map, restrictor):
    ts, zs, xs, ys, d, cols = source.shape
    assert ts == 1 and zs == 2
    sites, edge = zs * xs * ys, xs * ys
    slices, members = lax.axis_size("ta"), lax.axis_size("gz")
    forward, backward, out, back = routes(slices, members)
    t, g = lax.axis_index("ta"), lax.axis_index("gz")
    seam = jnp.where(t % GROUP == GROUP - 1, FORWARD_SEAM, jnp.where(t % GROUP == 0, BACKWARD_SEAM, 0))
    role = jnp.stack([jnp.where(g % 2 == 1, seam, 0), g]).astype(jnp.int32)

    b = source.reshape(sites, d, cols)
    selfs = self_codes.reshape(sites, d, d)
    hops = hop_codes.reshape(sites, d, 4 * d)
    restricts = restrictor.reshape(sites, -1, d)
    field = jax.ShapeDtypeStruct((sites, d, cols), BF16)
    wide = jax.ShapeDtypeStruct((sites, d, cols), F32)
    slab = jax.ShapeDtypeStruct((edge, d, cols), BF16)
    both = ("ta", "gz")

    scales = link_scales.astype(F32).reshape(sites * 5)
    t_terms, z_terms, detour = pl.pallas_call(
        hop_terms,
        out_shape=(field, slab, field),
        in_specs=[SMEM] * 2 + [VMEM] * 2,
        out_specs=(VMEM,) * 3,
        compiler_params=PARAMS,
    )(role, scales, b, hops)
    vector, estimate = b, b
    for sweep in range(ITERS):
        at_relay = lax.ppermute(detour, both, out)
        t_back = lax.ppermute(t_terms, both, forward)
        t_next = lax.ppermute(vector, both, backward)
        z_next = shifted(vector[:edge], "gz", -1)
        z_back = shifted(z_terms, "gz", 1)
        partial = pl.pallas_call(
            functools.partial(local_terms, (zs, xs, ys, d)),
            out_shape=wide,
            in_specs=[SMEM] + [VMEM] * 5,
            out_specs=VMEM,
            input_output_aliases={1: 0} if sweep else {},
            compiler_params=PARAMS,
        )(scales, estimate, b, vector, selfs, hops)
        relayed = lax.ppermute(at_relay, both, back)
        partial = pl.pallas_call(
            z_edge_terms,
            out_shape=wide,
            in_specs=[SMEM] + [VMEM] * 4,
            out_specs=VMEM,
            input_output_aliases={1: 0},
            compiler_params=PARAMS,
        )(scales, partial, z_next, z_back, hops)
        came = (partial, t_next, t_back, relayed, hops)
        if sweep + 1 < ITERS:
            estimate, vector, t_terms, z_terms, detour = pl.pallas_call(
                sweep_end,
                out_shape=(wide, field, field, slab, field),
                in_specs=[SMEM] * 2 + [VMEM] * 5,
                out_specs=(VMEM,) * 5,
                input_output_aliases={2: 0},
                compiler_params=PARAMS,
            )(role, scales, *came)
    keep = AGG // members
    coarse_d = restricts.shape[1]
    chunk = (keep, coarse_d, cols)
    pair = (2 * keep, coarse_d, cols)
    smoothed, own, away = pl.pallas_call(
        last_end,
        out_shape=(field, jax.ShapeDtypeStruct(pair, F32), jax.ShapeDtypeStruct(pair, BF16)),
        in_specs=[SMEM] * 3 + [VMEM] * 6,
        out_specs=(VMEM,) * 3,
        scratch_shapes=[pltpu.VMEM((AGG, coarse_d, cols), F32)],
        compiler_params=PARAMS,
    )(role, scales, restrict_map, *came, restricts)
    from_core = lax.ppermute(away, "gz", [(i, i ^ 1) for i in range(members)])
    mine, away = pl.pallas_call(
        coarse_step,
        out_shape=(jax.ShapeDtypeStruct(chunk, F32), jax.ShapeDtypeStruct(chunk, BF16)),
        in_specs=[SMEM] + [VMEM] * 2,
        out_specs=(VMEM,) * 2,
        compiler_params=PARAMS,
    )(role, own, from_core)
    from_chip = lax.ppermute(away, "gz", [(i, i ^ 2) for i in range(members)])
    coarse = mine + from_chip.astype(F32)
    return smoothed.reshape(source.shape), coarse.reshape(1, keep, coarse_d, cols)


def solution(mesh):
    site = P("ta", "gz", None, None, None, None)
    return jax.shard_map(
        shards,
        mesh=mesh,
        in_specs=(site, site, site, P("ta", "gz", None, None, None), P("ta", "gz", None, None), site),
        out_specs=(site, P("ta", "gz", None, None)),
        check_vma=False,
    )
```

```python
import functools

import jax
import jax.numpy as jnp
from jax import lax
from jax.experimental import pallas as pl
from jax.experimental.pallas import tpu as pltpu
from jax.sharding import PartitionSpec as P

ITERS = 3
OMEGA = 0.5
AGG = 16
F32 = jnp.float32
BF16 = jnp.bfloat16
VMEM = pl.BlockSpec(memory_space=pltpu.VMEM)
SMEM = pl.BlockSpec(memory_space=pltpu.SMEM)
PARAMS = pltpu.CompilerParams(vmem_limit_bytes=12 * 1024 * 1024)

GROUP = 32
FORWARD_RELAY = {1: 7, 3: 24}
BACKWARD_RELAY = {1: 24, 3: 7}


def routes(slices, members):
    inner, outer, out, back = [], [], [], []
    for t in range(slices):
        for g in range(members):
            here, ahead, behind = (((t + k) % slices) * members + g for k in (0, 1, -1))
            first = t // GROUP * GROUP
            inner.append((here, behind if t % 2 else ahead))
            across = ahead if t % 2 else behind
            relays = {GROUP - 1: FORWARD_RELAY, 0: BACKWARD_RELAY}.get(t % GROUP, {})
            if g in relays:
                relay = (first + relays[g]) * members + g
                out.append((here, relay))
                back.append((relay, across))
            else:
                outer.append((here, across))
    return inner, outer, out, back


def dot(a, b):
    return jnp.dot(a, b, preferred_element_type=F32)


def dot_t(a, b):
    return lax.dot_general(a, b, (((0,), (0,)), ((), ())), preferred_element_type=F32)


def either(parity, first, second):
    for value, pair in enumerate(((first, second), (second, first))):
        yield pl.when(parity == value), *pair


def hop_terms(role, scales, vector, hops, outer, inner, z_outer, z_inner, detour):
    sites, d = vector.shape[:2]
    edge = z_inner.shape[0]
    last = sites - edge
    for when, ahead, behind in either(role[2], inner, outer):

        @when
        def _():
            for s in range(sites):
                ahead[s] = (scales[5 * s + 4] * dot_t(hops[s, :, 3 * d :], vector[s])).astype(BF16)
            behind[...] = vector[...]

    for when, ahead, behind in either(role[3], z_inner, z_outer):

        @when
        def _():
            for s in range(last, sites):
                ahead[s - last] = (scales[5 * s + 3] * dot_t(hops[s, :, 2 * d : 3 * d], vector[s])).astype(BF16)
            behind[...] = vector[:edge]

    @pl.when(role[0] != 0)
    def _():
        detour[...] = outer[...]


def local_terms(shape, scales, estimate, source, vector, selfs, hops, partial):
    zs, xs, ys, d = shape

    def at(z, x, y):
        return (z * xs + x % xs) * ys + y % ys

    def fwd(m, s, p):
        return scales[5 * s + m + 1] * dot(hops[s, :, m * d : (m + 1) * d], p)

    def bwd(m, s):
        return scales[5 * s + m + 1] * dot_t(hops[s, :, m * d : (m + 1) * d], vector[s])

    for z in range(zs):
        for x in range(xs):
            for y in range(ys):
                s = at(z, x, y)
                p = vector[s]
                total = p.astype(F32) + scales[5 * s] * dot(selfs[s], p)
                total += fwd(0, s, vector[at(z, x + 1, y)])
                total += fwd(1, s, vector[at(z, x, y + 1)])
                total += bwd(0, at(z, x - 1, y))
                total += bwd(1, at(z, x, y - 1))
                if z + 1 < zs:
                    total += fwd(2, s, vector[at(z + 1, x, y)])
                if z:
                    total += bwd(2, at(z - 1, x, y))
                partial[s] = estimate[s].astype(F32) + OMEGA * (source[s].astype(F32) - total)


def z_edge_terms(role, scales, partial, z_inner, z_outer, hops, done):
    sites, d = partial.shape[:2]
    edge = z_inner.shape[0]
    last = sites - edge
    for when, z_next, z_back in either(role[3], z_inner, z_outer):

        @when
        def _():
            for s in range(edge):
                done[s] = partial[s] - OMEGA * z_back[s].astype(F32)
            for s in range(last, sites):
                term = dot(hops[s, :, 2 * d : 3 * d], z_next[s - last])
                done[s] = partial[s] - OMEGA * scales[5 * s + 3] * term


def new_estimates(role, scales, partial, inner, outer, relayed, hops, store):
    sites, d = partial.shape[:2]
    for when, t_next, t_back in either(role[2], inner, outer):

        @when
        def _():
            for s in range(sites):
                came = [jnp.where(role[0] != 0, relayed[s], ref[s]) if ref is outer else ref[s] for ref in (t_next, t_back)]
                total = scales[5 * s + 4] * dot(hops[s, :, 3 * d :], came[0]) + came[1].astype(F32)
                store(s, partial[s] - OMEGA * total)


def sweep_end(role, scales, partial, inner, outer, relayed, hops, estimate, vector, *messages):
    def store(s, e):
        estimate[s] = e
        vector[s] = e.astype(BF16)

    new_estimates(role, scales, partial, inner, outer, relayed, hops, store)
    hop_terms(role, scales, vector, hops, *messages)


def last_end(role, scales, labels, partial, inner, outer, relayed, hops, restrictor, vector, own, away, sums):
    half = own.shape[0] // 2
    xs, ys = labels.shape[2:]
    sums[...] = jnp.zeros_like(sums)

    def store(s, e):
        vector[s] = e.astype(BF16)

    new_estimates(role, scales, partial, inner, outer, relayed, hops, store)
    for s in range(vector.shape[0]):
        label = labels[0, s // (xs * ys), s // ys % xs, s % ys]
        sums[label] += dot(restrictor[s], vector[s])
    core = role[3]
    for chip in range(2):
        rows = pl.ds(chip * half, half)
        own[rows] = sums[pl.ds((2 * chip + core) * half, half)]
        away[rows] = sums[pl.ds((2 * chip + 1 - core) * half, half)].astype(BF16)


def coarse_step(role, own, came, mine, away):
    half = mine.shape[0]
    chip = role[1] // 2
    here, there = pl.ds(chip * half, half), pl.ds((1 - chip) * half, half)
    mine[...] = own[here] + came[here].astype(F32)
    away[...] = (own[there] + came[there].astype(F32)).astype(BF16)


def shards(source, self_codes, hop_codes, link_scales, restrict_map, restrictor):
    ts, zs, xs, ys, d, cols = source.shape
    assert ts == 1 and zs == 2
    sites, edge = zs * xs * ys, xs * ys
    slices, members = lax.axis_size("ta"), lax.axis_size("gz")
    inner, outer, out, back = routes(slices, members)
    z_inner = [(i, i ^ 1) for i in range(members)]
    z_outer = [(i, (i + 2 * (i % 2) - 1) % members) for i in range(members)]
    t, g = lax.axis_index("ta"), lax.axis_index("gz")
    seam = jnp.logical_or(t % GROUP == GROUP - 1, t % GROUP == 0)
    role = jnp.stack([jnp.logical_and(g % 2 == 1, seam).astype(jnp.int32), g, t % 2, g % 2]).astype(jnp.int32)

    b = source.reshape(sites, d, cols)
    selfs = self_codes.reshape(sites, d, d)
    hops = hop_codes.reshape(sites, d, 4 * d)
    restricts = restrictor.reshape(sites, -1, d)
    field = jax.ShapeDtypeStruct((sites, d, cols), BF16)
    wide = jax.ShapeDtypeStruct((sites, d, cols), F32)
    slab = jax.ShapeDtypeStruct((edge, d, cols), BF16)
    both = ("ta", "gz")

    scales = link_scales.astype(F32).reshape(sites * 5)
    messages = (field, field, slab, slab, field)
    sent = pl.pallas_call(
        hop_terms,
        out_shape=messages,
        in_specs=[SMEM] * 2 + [VMEM] * 2,
        out_specs=(VMEM,) * 5,
        compiler_params=PARAMS,
    )(role, scales, b, hops)
    vector, estimate = b, b
    for sweep in range(ITERS):
        at_relay = lax.ppermute(sent[4], both, out)
        t_outer = lax.ppermute(sent[0], both, outer)
        t_inner = lax.ppermute(sent[1], both, inner)
        from_z_outer = lax.ppermute(sent[2], "gz", z_outer)
        from_z_inner = lax.ppermute(sent[3], "gz", z_inner)
        partial = pl.pallas_call(
            functools.partial(local_terms, (zs, xs, ys, d)),
            out_shape=wide,
            in_specs=[SMEM] + [VMEM] * 5,
            out_specs=VMEM,
            input_output_aliases={1: 0} if sweep else {},
            compiler_params=PARAMS,
        )(scales, estimate, b, vector, selfs, hops)
        relayed = lax.ppermute(at_relay, both, back)
        partial = pl.pallas_call(
            z_edge_terms,
            out_shape=wide,
            in_specs=[SMEM] * 2 + [VMEM] * 4,
            out_specs=VMEM,
            input_output_aliases={2: 0},
            compiler_params=PARAMS,
        )(role, scales, partial, from_z_inner, from_z_outer, hops)
        came = (partial, t_inner, t_outer, relayed, hops)
        if sweep + 1 < ITERS:
            estimate, vector, *sent = pl.pallas_call(
                sweep_end,
                out_shape=(wide, field) + messages,
                in_specs=[SMEM] * 2 + [VMEM] * 5,
                out_specs=(VMEM,) * 7,
                input_output_aliases={2: 0},
                compiler_params=PARAMS,
            )(role, scales, *came)
    keep = AGG // members
    coarse_d = restricts.shape[1]
    chunk = (keep, coarse_d, cols)
    pair = (2 * keep, coarse_d, cols)
    smoothed, own, away = pl.pallas_call(
        last_end,
        out_shape=(field, jax.ShapeDtypeStruct(pair, F32), jax.ShapeDtypeStruct(pair, BF16)),
        in_specs=[SMEM] * 3 + [VMEM] * 6,
        out_specs=(VMEM,) * 3,
        scratch_shapes=[pltpu.VMEM((AGG, coarse_d, cols), F32)],
        compiler_params=PARAMS,
    )(role, scales, restrict_map, *came, restricts)
    from_core = lax.ppermute(away, "gz", [(i, i ^ 1) for i in range(members)])
    mine, away = pl.pallas_call(
        coarse_step,
        out_shape=(jax.ShapeDtypeStruct(chunk, F32), jax.ShapeDtypeStruct(chunk, BF16)),
        in_specs=[SMEM] + [VMEM] * 2,
        out_specs=(VMEM,) * 2,
        compiler_params=PARAMS,
    )(role, own, from_core)
    from_chip = lax.ppermute(away, "gz", [(i, i ^ 2) for i in range(members)])
    coarse = mine + from_chip.astype(F32)
    return smoothed.reshape(source.shape), coarse.reshape(1, keep, coarse_d, cols)


def solution(mesh):
    site = P("ta", "gz", None, None, None, None)
    return jax.shard_map(
        shards,
        mesh=mesh,
        in_specs=(site, site, site, P("ta", "gz", None, None, None), P("ta", "gz", None, None), site),
        out_specs=(site, P("ta", "gz", None, None)),
        check_vma=False,
    )
```

```python
import functools

import jax
import jax.numpy as jnp
from jax import lax
from jax.experimental import pallas as pl
from jax.experimental.pallas import tpu as pltpu
from jax.sharding import PartitionSpec as P

ITERS = 3
OMEGA = 0.5
AGG = 16
F32 = jnp.float32
BF16 = jnp.bfloat16
VMEM = pl.BlockSpec(memory_space=pltpu.VMEM)
SMEM = pl.BlockSpec(memory_space=pltpu.SMEM)
LONG = pl.CostEstimate(flops=10_000_000_000, bytes_accessed=0, transcendentals=0)
PARAMS = pltpu.CompilerParams(vmem_limit_bytes=12 * 1024 * 1024)

GROUP = 32
FORWARD_RELAY = {1: 7, 3: 24}
BACKWARD_RELAY = {1: 24, 3: 7}


def routes(slices, members):
    inner, outer, out, back = [], [], [], []
    for t in range(slices):
        for g in range(members):
            here, ahead, behind = (((t + k) % slices) * members + g for k in (0, 1, -1))
            first = t // GROUP * GROUP
            inner.append((here, behind if t % 2 else ahead))
            across = ahead if t % 2 else behind
            relays = {GROUP - 1: FORWARD_RELAY, 0: BACKWARD_RELAY}.get(t % GROUP, {})
            if g in relays:
                relay = (first + relays[g]) * members + g
                out.append((here, relay))
                back.append((relay, across))
            else:
                outer.append((here, across))
    return inner, outer, out, back


def dot(a, b):
    return jnp.dot(a, b, preferred_element_type=F32)


def dot_t(a, b):
    return lax.dot_general(a, b, (((0,), (0,)), ((), ())), preferred_element_type=F32)


def either(parity, first, second):
    for value, pair in enumerate(((first, second), (second, first))):
        yield pl.when(parity == value), *pair


def hop_terms(role, scales, vector, hops, outer, inner, z_outer, z_inner, detour):
    sites, d = vector.shape[:2]
    edge = z_inner.shape[0]
    last = sites - edge
    for when, ahead, behind in either(role[2], inner, outer):

        @when
        def _():
            for s in range(sites):
                ahead[s] = (scales[5 * s + 4] * dot_t(hops[s, :, 3 * d :], vector[s])).astype(BF16)
            behind[...] = vector[...]

    for when, ahead, behind in either(role[3], z_inner, z_outer):

        @when
        def _():
            for s in range(last, sites):
                ahead[s - last] = (scales[5 * s + 3] * dot_t(hops[s, :, 2 * d : 3 * d], vector[s])).astype(BF16)
            behind[...] = vector[:edge]

    @pl.when(role[0] != 0)
    def _():
        detour[...] = outer[...]


def local_terms(shape, scales, estimate, source, vector, selfs, hops, partial):
    zs, xs, ys, d = shape

    def at(z, x, y):
        return (z * xs + x % xs) * ys + y % ys

    def fwd(m, s, p):
        return scales[5 * s + m + 1] * dot(hops[s, :, m * d : (m + 1) * d], p)

    def bwd(m, s):
        return scales[5 * s + m + 1] * dot_t(hops[s, :, m * d : (m + 1) * d], vector[s])

    for z in range(zs):
        for x in range(xs):
            for y in range(ys):
                s = at(z, x, y)
                p = vector[s]
                total = p.astype(F32) + scales[5 * s] * dot(selfs[s], p)
                total += fwd(0, s, vector[at(z, x + 1, y)])
                total += fwd(1, s, vector[at(z, x, y + 1)])
                total += bwd(0, at(z, x - 1, y))
                total += bwd(1, at(z, x, y - 1))
                if z + 1 < zs:
                    total += fwd(2, s, vector[at(z + 1, x, y)])
                if z:
                    total += bwd(2, at(z - 1, x, y))
                partial[s] = estimate[s].astype(F32) + OMEGA * (source[s].astype(F32) - total)


def z_edge_terms(role, scales, partial, z_inner, z_outer, hops, done):
    sites, d = partial.shape[:2]
    edge = z_inner.shape[0]
    last = sites - edge
    for when, z_next, z_back in either(role[3], z_inner, z_outer):

        @when
        def _():
            for s in range(edge):
                done[s] = partial[s] - OMEGA * z_back[s].astype(F32)
            for s in range(last, sites):
                term = dot(hops[s, :, 2 * d : 3 * d], z_next[s - last])
                done[s] = partial[s] - OMEGA * scales[5 * s + 3] * term


def new_estimates(role, scales, relayed, outer, inner, partial, hops, store):
    sites, d = partial.shape[:2]
    for when, t_next, t_back in either(role[2], inner, outer):

        @when
        def _():
            for s in range(sites):
                came = [jnp.where(role[0] != 0, relayed[s], ref[s]) if ref is outer else ref[s] for ref in (t_next, t_back)]
                total = scales[5 * s + 4] * dot(hops[s, :, 3 * d :], came[0]) + came[1].astype(F32)
                store(s, partial[s] - OMEGA * total)


def sweep_end(role, scales, relayed, outer, inner, partial, hops, estimate, vector, *messages):
    def store(s, e):
        estimate[s] = e
        vector[s] = e.astype(BF16)

    new_estimates(role, scales, relayed, outer, inner, partial, hops, store)
    hop_terms(role, scales, vector, hops, *messages)


def last_end(role, scales, labels, relayed, outer, inner, partial, hops, restrictor, vector, own, away, sums):
    half = own.shape[0] // 2
    xs, ys = labels.shape[2:]
    sums[...] = jnp.zeros_like(sums)

    def store(s, e):
        vector[s] = e.astype(BF16)

    new_estimates(role, scales, relayed, outer, inner, partial, hops, store)
    for s in range(vector.shape[0]):
        label = labels[0, s // (xs * ys), s // ys % xs, s % ys]
        sums[label] += dot(restrictor[s], vector[s])
    core = role[3]
    for chip in range(2):
        rows = pl.ds(chip * half, half)
        own[rows] = sums[pl.ds((2 * chip + core) * half, half)]
        away[rows] = sums[pl.ds((2 * chip + 1 - core) * half, half)].astype(BF16)


def coarse_step(role, own, came, mine, away):
    half = mine.shape[0]
    chip = role[1] // 2
    here, there = pl.ds(chip * half, half), pl.ds((1 - chip) * half, half)
    mine[...] = own[here] + came[here].astype(F32)
    away[...] = (own[there] + came[there].astype(F32)).astype(BF16)


def shards(source, self_codes, hop_codes, link_scales, restrict_map, restrictor):
    ts, zs, xs, ys, d, cols = source.shape
    assert ts == 1 and zs == 2
    sites, edge = zs * xs * ys, xs * ys
    slices, members = lax.axis_size("ta"), lax.axis_size("gz")
    inner, outer, out, back = routes(slices, members)
    z_inner = [(i, i ^ 1) for i in range(members)]
    z_outer = [(i, (i + 2 * (i % 2) - 1) % members) for i in range(members)]
    t, g = lax.axis_index("ta"), lax.axis_index("gz")
    seam = jnp.logical_or(t % GROUP == GROUP - 1, t % GROUP == 0)
    role = jnp.stack([jnp.logical_and(g % 2 == 1, seam).astype(jnp.int32), g, t % 2, g % 2]).astype(jnp.int32)

    b = source.reshape(sites, d, cols)
    selfs = self_codes.reshape(sites, d, d)
    hops = hop_codes.reshape(sites, d, 4 * d)
    restricts = restrictor.reshape(sites, -1, d)
    field = jax.ShapeDtypeStruct((sites, d, cols), BF16)
    wide = jax.ShapeDtypeStruct((sites, d, cols), F32)
    slab = jax.ShapeDtypeStruct((edge, d, cols), BF16)
    both = ("ta", "gz")

    scales = link_scales.astype(F32).reshape(sites * 5)
    messages = (field, field, slab, slab, field)
    sent = pl.pallas_call(
        hop_terms,
        out_shape=messages,
        in_specs=[SMEM] * 2 + [VMEM] * 2,
        out_specs=(VMEM,) * 5,
        compiler_params=PARAMS,
    )(role, scales, b, hops)
    vector, estimate = b, b
    for sweep in range(ITERS):
        at_relay = lax.ppermute(sent[4], both, out)
        t_outer = lax.ppermute(sent[0], both, outer)
        t_inner = lax.ppermute(sent[1], both, inner)
        from_z_outer = lax.ppermute(sent[2], "gz", z_outer)
        from_z_inner = lax.ppermute(sent[3], "gz", z_inner)
        partial = pl.pallas_call(
            functools.partial(local_terms, (zs, xs, ys, d)),
            out_shape=wide,
            in_specs=[SMEM] + [VMEM] * 5,
            out_specs=VMEM,
            input_output_aliases={1: 0} if sweep else {},
            cost_estimate=LONG,
            compiler_params=PARAMS,
        )(scales, estimate, b, vector, selfs, hops)
        relayed = lax.ppermute(at_relay, both, back)
        partial = pl.pallas_call(
            z_edge_terms,
            out_shape=wide,
            in_specs=[SMEM] * 2 + [VMEM] * 4,
            out_specs=VMEM,
            input_output_aliases={2: 0},
            compiler_params=PARAMS,
        )(role, scales, partial, from_z_inner, from_z_outer, hops)
        came = (relayed, t_outer, t_inner, partial, hops)
        if sweep + 1 < ITERS:
            estimate, vector, *sent = pl.pallas_call(
                sweep_end,
                out_shape=(wide, field) + messages,
                in_specs=[SMEM] * 2 + [VMEM] * 5,
                out_specs=(VMEM,) * 7,
                input_output_aliases={5: 0},
                compiler_params=PARAMS,
            )(role, scales, *came)
    keep = AGG // members
    coarse_d = restricts.shape[1]
    chunk = (keep, coarse_d, cols)
    pair = (2 * keep, coarse_d, cols)
    smoothed, own, away = pl.pallas_call(
        last_end,
        out_shape=(field, jax.ShapeDtypeStruct(pair, F32), jax.ShapeDtypeStruct(pair, BF16)),
        in_specs=[SMEM] * 3 + [VMEM] * 6,
        out_specs=(VMEM,) * 3,
        scratch_shapes=[pltpu.VMEM((AGG, coarse_d, cols), F32)],
        compiler_params=PARAMS,
    )(role, scales, restrict_map, *came, restricts)
    from_core = lax.ppermute(away, "gz", [(i, i ^ 1) for i in range(members)])
    mine, away = pl.pallas_call(
        coarse_step,
        out_shape=(jax.ShapeDtypeStruct(chunk, F32), jax.ShapeDtypeStruct(chunk, BF16)),
        in_specs=[SMEM] + [VMEM] * 2,
        out_specs=(VMEM,) * 2,
        compiler_params=PARAMS,
    )(role, own, from_core)
    from_chip = lax.ppermute(away, "gz", [(i, i ^ 2) for i in range(members)])
    coarse = mine + from_chip.astype(F32)
    return smoothed.reshape(source.shape), coarse.reshape(1, keep, coarse_d, cols)


def solution(mesh):
    site = P("ta", "gz", None, None, None, None)
    return jax.shard_map(
        shards,
        mesh=mesh,
        in_specs=(site, site, site, P("ta", "gz", None, None, None), P("ta", "gz", None, None), site),
        out_specs=(site, P("ta", "gz", None, None)),
        check_vma=False,
    )
```

```python
import functools

import jax
import jax.numpy as jnp
from jax import lax
from jax.experimental import pallas as pl
from jax.experimental.pallas import tpu as pltpu
from jax.sharding import PartitionSpec as P

ITERS = 3
OMEGA = 0.5
AGG = 16
F32 = jnp.float32
BF16 = jnp.bfloat16
VMEM = pl.BlockSpec(memory_space=pltpu.VMEM)
SMEM = pl.BlockSpec(memory_space=pltpu.SMEM)
PARAMS = pltpu.CompilerParams(vmem_limit_bytes=12 * 1024 * 1024)

GROUP = 32
FORWARD_RELAY = {1: 7, 3: 24}
BACKWARD_RELAY = {1: 24, 3: 7}


def routes(slices, members):
    inner, outer, out, back = [], [], [], []
    for t in range(slices):
        for g in range(members):
            here, ahead, behind = (((t + k) % slices) * members + g for k in (0, 1, -1))
            first = t // GROUP * GROUP
            inner.append((here, behind if t % 2 else ahead))
            across = ahead if t % 2 else behind
            relays = {GROUP - 1: FORWARD_RELAY, 0: BACKWARD_RELAY}.get(t % GROUP, {})
            if g in relays:
                relay = (first + relays[g]) * members + g
                out.append((here, relay))
                back.append((relay, across))
            else:
                outer.append((here, across))
    return inner, outer, out, back


def dot(a, b):
    return jnp.dot(a, b, preferred_element_type=F32)


def dot_t(a, b):
    return lax.dot_general(a, b, (((0,), (0,)), ((), ())), preferred_element_type=F32)


def either(parity, first, second):
    for value, pair in enumerate(((first, second), (second, first))):
        yield pl.when(parity == value), *pair


def hop_terms(role, scales, vector, hops, outer, inner, z_outer, z_inner, detour):
    sites, d = vector.shape[:2]
    edge = z_inner.shape[0]
    last = sites - edge
    for when, ahead, behind in either(role[2], inner, outer):

        @when
        def _():
            for s in range(sites):
                ahead[s] = (scales[5 * s + 4] * dot_t(hops[s, :, 3 * d :], vector[s])).astype(BF16)
            behind[...] = vector[...]

    for when, ahead, behind in either(role[3], z_inner, z_outer):

        @when
        def _():
            for s in range(last, sites):
                ahead[s - last] = (scales[5 * s + 3] * dot_t(hops[s, :, 2 * d : 3 * d], vector[s])).astype(BF16)
            behind[...] = vector[:edge]

    @pl.when(role[0] != 0)
    def _():
        detour[...] = outer[...]


def local_terms(shape, scales, estimate, source, vector, selfs, hops, partial):
    zs, xs, ys, d = shape

    def at(z, x, y):
        return (z * xs + x % xs) * ys + y % ys

    def fwd(m, s, p):
        return scales[5 * s + m + 1] * dot(hops[s, :, m * d : (m + 1) * d], p)

    def bwd(m, s):
        return scales[5 * s + m + 1] * dot_t(hops[s, :, m * d : (m + 1) * d], vector[s])

    for z in range(zs):
        for x in range(xs):
            for y in range(ys):
                s = at(z, x, y)
                p = vector[s]
                total = p.astype(F32) + scales[5 * s] * dot(selfs[s], p)
                total += fwd(0, s, vector[at(z, x + 1, y)])
                total += fwd(1, s, vector[at(z, x, y + 1)])
                total += bwd(0, at(z, x - 1, y))
                total += bwd(1, at(z, x, y - 1))
                if z + 1 < zs:
                    total += fwd(2, s, vector[at(z + 1, x, y)])
                if z:
                    total += bwd(2, at(z - 1, x, y))
                partial[s] = estimate[s].astype(F32) + OMEGA * (source[s].astype(F32) - total)


def z_edge_terms(role, scales, partial, z_inner, z_outer, hops, done):
    sites, d = partial.shape[:2]
    edge = z_inner.shape[0]
    last = sites - edge
    for when, z_next, z_back in either(role[3], z_inner, z_outer):

        @when
        def _():
            for s in range(edge):
                done[s] = partial[s] - OMEGA * z_back[s].astype(F32)
            for s in range(last, sites):
                term = dot(hops[s, :, 2 * d : 3 * d], z_next[s - last])
                done[s] = partial[s] - OMEGA * scales[5 * s + 3] * term


def new_estimates(role, scales, relayed, outer, inner, partial, hops, store):
    sites, d = partial.shape[:2]
    for when, t_next, t_back in either(role[2], inner, outer):

        @when
        def _():
            for s in range(sites):
                came = [jnp.where(role[0] != 0, relayed[s], ref[s]) if ref is outer else ref[s] for ref in (t_next, t_back)]
                total = scales[5 * s + 4] * dot(hops[s, :, 3 * d :], came[0]) + came[1].astype(F32)
                store(s, partial[s] - OMEGA * total)


def sweep_end(role, scales, relayed, outer, inner, partial, hops, estimate, vector, *messages):
    def store(s, e):
        estimate[s] = e
        vector[s] = e.astype(BF16)

    new_estimates(role, scales, relayed, outer, inner, partial, hops, store)
    hop_terms(role, scales, vector, hops, *messages)


def last_end(role, scales, labels, relayed, outer, inner, partial, hops, restrictor, vector, own, away, sums):
    half = own.shape[0] // 2
    xs, ys = labels.shape[2:]
    sums[...] = jnp.zeros_like(sums)

    def store(s, e):
        vector[s] = e.astype(BF16)

    new_estimates(role, scales, relayed, outer, inner, partial, hops, store)
    for s in range(vector.shape[0]):
        label = labels[0, s // (xs * ys), s // ys % xs, s % ys]
        sums[label] += dot(restrictor[s], vector[s])
    core = role[3]
    for chip in range(2):
        rows = pl.ds(chip * half, half)
        own[rows] = sums[pl.ds((2 * chip + core) * half, half)]
        away[rows] = sums[pl.ds((2 * chip + 1 - core) * half, half)].astype(BF16)


def coarse_step(role, own, came, mine, away):
    half = mine.shape[0]
    chip = role[1] // 2
    here, there = pl.ds(chip * half, half), pl.ds((1 - chip) * half, half)
    mine[...] = own[here] + came[here].astype(F32)
    away[...] = (own[there] + came[there].astype(F32)).astype(BF16)


def shards(source, self_codes, hop_codes, link_scales, restrict_map, restrictor):
    ts, zs, xs, ys, d, cols = source.shape
    assert ts == 1 and zs == 2
    sites, edge = zs * xs * ys, xs * ys
    slices, members = lax.axis_size("ta"), lax.axis_size("gz")
    inner, outer, out, back = routes(slices, members)
    z_inner = [(i, i ^ 1) for i in range(members)]
    z_outer = [(i, (i + 2 * (i % 2) - 1) % members) for i in range(members)]
    t, g = lax.axis_index("ta"), lax.axis_index("gz")
    seam = jnp.logical_or(t % GROUP == GROUP - 1, t % GROUP == 0)
    role = jnp.stack([jnp.logical_and(g % 2 == 1, seam).astype(jnp.int32), g, t % 2, g % 2]).astype(jnp.int32)

    b = source.reshape(sites, d, cols)
    selfs = self_codes.reshape(sites, d, d)
    hops = hop_codes.reshape(sites, d, 4 * d)
    restricts = restrictor.reshape(sites, -1, d)
    field = jax.ShapeDtypeStruct((sites, d, cols), BF16)
    wide = jax.ShapeDtypeStruct((sites, d, cols), F32)
    slab = jax.ShapeDtypeStruct((edge, d, cols), BF16)
    both = ("ta", "gz")

    scales = link_scales.astype(F32).reshape(sites * 5)
    messages = (field, field, slab, slab, field)
    sent = pl.pallas_call(
        hop_terms,
        out_shape=messages,
        in_specs=[SMEM] * 2 + [VMEM] * 2,
        out_specs=(VMEM,) * 5,
        compiler_params=PARAMS,
    )(role, scales, b, hops)
    vector, estimate = b, b
    for sweep in range(ITERS):
        at_relay = lax.ppermute(sent[4], both, out)
        t_outer = lax.ppermute(sent[0], both, outer)
        t_inner = lax.ppermute(sent[1], both, inner)
        from_z_outer = lax.ppermute(sent[2], "gz", z_outer)
        from_z_inner = lax.ppermute(sent[3], "gz", z_inner)
        partial = pl.pallas_call(
            functools.partial(local_terms, (zs, xs, ys, d)),
            out_shape=wide,
            in_specs=[SMEM] + [VMEM] * 5,
            out_specs=VMEM,
            input_output_aliases={1: 0} if sweep else {},
            compiler_params=PARAMS,
        )(scales, estimate, b, vector, selfs, hops)
        relayed = lax.ppermute(at_relay, both, back)
        partial = pl.pallas_call(
            z_edge_terms,
            out_shape=wide,
            in_specs=[SMEM] * 2 + [VMEM] * 4,
            out_specs=VMEM,
            input_output_aliases={2: 0},
            compiler_params=PARAMS,
        )(role, scales, partial, from_z_inner, from_z_outer, hops)
        came = (relayed, t_outer, t_inner, partial, hops)
        if sweep + 1 < ITERS:
            estimate, vector, *sent = pl.pallas_call(
                sweep_end,
                out_shape=(wide, field) + messages,
                in_specs=[SMEM] * 2 + [VMEM] * 5,
                out_specs=(VMEM,) * 7,
                input_output_aliases={5: 0},
                compiler_params=PARAMS,
            )(role, scales, *came)
    keep = AGG // members
    coarse_d = restricts.shape[1]
    chunk = (keep, coarse_d, cols)
    pair = (2 * keep, coarse_d, cols)
    smoothed, own, away = pl.pallas_call(
        last_end,
        out_shape=(field, jax.ShapeDtypeStruct(pair, F32), jax.ShapeDtypeStruct(pair, BF16)),
        in_specs=[SMEM] * 3 + [VMEM] * 6,
        out_specs=(VMEM,) * 3,
        scratch_shapes=[pltpu.VMEM((AGG, coarse_d, cols), F32)],
        compiler_params=PARAMS,
    )(role, scales, restrict_map, *came, restricts)
    from_core = lax.ppermute(away, "gz", [(i, i ^ 1) for i in range(members)])
    mine, away = pl.pallas_call(
        coarse_step,
        out_shape=(jax.ShapeDtypeStruct(chunk, F32), jax.ShapeDtypeStruct(chunk, BF16)),
        in_specs=[SMEM] + [VMEM] * 2,
        out_specs=(VMEM,) * 2,
        compiler_params=PARAMS,
    )(role, own, from_core)
    from_chip = lax.ppermute(away, "gz", [(i, i ^ 2) for i in range(members)])
    coarse = mine + from_chip.astype(F32)
    return smoothed.reshape(source.shape), coarse.reshape(1, keep, coarse_d, cols)


def solution(mesh):
    site = P("ta", "gz", None, None, None, None)
    return jax.shard_map(
        shards,
        mesh=mesh,
        in_specs=(site, site, site, P("ta", "gz", None, None, None), P("ta", "gz", None, None), site),
        out_specs=(site, P("ta", "gz", None, None)),
        check_vma=False,
    )
```

```python
import functools

import jax
import jax.numpy as jnp
from jax import lax
from jax.experimental import pallas as pl
from jax.experimental.pallas import tpu as pltpu
from jax.sharding import PartitionSpec as P

ITERS = 3
OMEGA = 0.5
AGG = 16
F32 = jnp.float32
BF16 = jnp.bfloat16
VMEM = pl.BlockSpec(memory_space=pltpu.VMEM)
SMEM = pl.BlockSpec(memory_space=pltpu.SMEM)
LONG = pl.CostEstimate(flops=10_000_000_000, bytes_accessed=0, transcendentals=0)
PARAMS = pltpu.CompilerParams(vmem_limit_bytes=12 * 1024 * 1024)

GROUP = 32
FORWARD_RELAY = {1: 7, 3: 24}
BACKWARD_RELAY = {1: 24, 3: 7}


def routes(slices, members):
    inner, outer, out, back = [], [], [], []
    for t in range(slices):
        for g in range(members):
            here, ahead, behind = (((t + k) % slices) * members + g for k in (0, 1, -1))
            first = t // GROUP * GROUP
            inner.append((here, behind if t % 2 else ahead))
            across = ahead if t % 2 else behind
            relays = {GROUP - 1: FORWARD_RELAY, 0: BACKWARD_RELAY}.get(t % GROUP, {})
            if g in relays:
                relay = (first + relays[g]) * members + g
                out.append((here, relay))
                back.append((relay, across))
            else:
                outer.append((here, across))
    return inner, outer, out, back


def dot(a, b):
    return jnp.dot(a, b, preferred_element_type=F32)


def dot_t(a, b):
    return lax.dot_general(a, b, (((0,), (0,)), ((), ())), preferred_element_type=F32)


def either(parity, first, second):
    for value, pair in enumerate(((first, second), (second, first))):
        yield pl.when(parity == value), *pair


def hop_terms(role, scales, vector, hops, outer, inner, z_outer, z_inner, detour):
    sites, d = vector.shape[:2]
    edge = z_inner.shape[0]
    last = sites - edge
    for when, ahead, behind in either(role[2], inner, outer):

        @when
        def _():
            for s in range(sites):
                ahead[s] = (scales[5 * s + 4] * dot_t(hops[s, :, 3 * d :], vector[s])).astype(BF16)
            behind[...] = vector[...]

    for when, ahead, behind in either(role[3], z_inner, z_outer):

        @when
        def _():
            for s in range(last, sites):
                ahead[s - last] = (scales[5 * s + 3] * dot_t(hops[s, :, 2 * d : 3 * d], vector[s])).astype(BF16)
            behind[...] = vector[:edge]

    @pl.when(role[0] != 0)
    def _():
        detour[...] = outer[...]


def local_terms(shape, scales, estimate, source, vector, selfs, hops, partial):
    zs, xs, ys, d = shape

    def at(z, x, y):
        return (z * xs + x % xs) * ys + y % ys

    def fwd(m, s, p):
        return scales[5 * s + m + 1] * dot(hops[s, :, m * d : (m + 1) * d], p)

    def bwd(m, s):
        return scales[5 * s + m + 1] * dot_t(hops[s, :, m * d : (m + 1) * d], vector[s])

    for z in range(zs):
        for x in range(xs):
            for y in range(ys):
                s = at(z, x, y)
                p = vector[s]
                total = p.astype(F32) + scales[5 * s] * dot(selfs[s], p)
                total += fwd(0, s, vector[at(z, x + 1, y)])
                total += fwd(1, s, vector[at(z, x, y + 1)])
                total += bwd(0, at(z, x - 1, y))
                total += bwd(1, at(z, x, y - 1))
                if z + 1 < zs:
                    total += fwd(2, s, vector[at(z + 1, x, y)])
                if z:
                    total += bwd(2, at(z - 1, x, y))
                partial[s] = estimate[s].astype(F32) + OMEGA * (source[s].astype(F32) - total)


def z_edge_terms(role, scales, partial, z_inner, z_outer, hops, done):
    sites, d = partial.shape[:2]
    edge = z_inner.shape[0]
    last = sites - edge
    for when, z_next, z_back in either(role[3], z_inner, z_outer):

        @when
        def _():
            for s in range(edge):
                done[s] = partial[s] - OMEGA * z_back[s].astype(F32)
            for s in range(last, sites):
                term = dot(hops[s, :, 2 * d : 3 * d], z_next[s - last])
                done[s] = partial[s] - OMEGA * scales[5 * s + 3] * term


def new_estimates(role, scales, partial, inner, outer, relayed, hops, store):
    sites, d = partial.shape[:2]
    for when, t_next, t_back in either(role[2], inner, outer):

        @when
        def _():
            for s in range(sites):
                came = [jnp.where(role[0] != 0, relayed[s], ref[s]) if ref is outer else ref[s] for ref in (t_next, t_back)]
                total = scales[5 * s + 4] * dot(hops[s, :, 3 * d :], came[0]) + came[1].astype(F32)
                store(s, partial[s] - OMEGA * total)


def sweep_end(role, scales, partial, inner, outer, relayed, hops, estimate, vector, *messages):
    def store(s, e):
        estimate[s] = e
        vector[s] = e.astype(BF16)

    new_estimates(role, scales, partial, inner, outer, relayed, hops, store)
    hop_terms(role, scales, vector, hops, *messages)


def last_end(role, scales, labels, partial, inner, outer, relayed, hops, restrictor, vector, own, away, sums):
    half = own.shape[0] // 2
    xs, ys = labels.shape[2:]
    sums[...] = jnp.zeros_like(sums)

    def store(s, e):
        vector[s] = e.astype(BF16)

    new_estimates(role, scales, partial, inner, outer, relayed, hops, store)
    for s in range(vector.shape[0]):
        label = labels[0, s // (xs * ys), s // ys % xs, s % ys]
        sums[label] += dot(restrictor[s], vector[s])
    core = role[3]
    for chip in range(2):
        rows = pl.ds(chip * half, half)
        own[rows] = sums[pl.ds((2 * chip + core) * half, half)]
        away[rows] = sums[pl.ds((2 * chip + 1 - core) * half, half)].astype(BF16)


def coarse_step(role, own, came, mine, away):
    half = mine.shape[0]
    chip = role[1] // 2
    here, there = pl.ds(chip * half, half), pl.ds((1 - chip) * half, half)
    mine[...] = own[here] + came[here].astype(F32)
    away[...] = (own[there] + came[there].astype(F32)).astype(BF16)


def shards(source, self_codes, hop_codes, link_scales, restrict_map, restrictor):
    ts, zs, xs, ys, d, cols = source.shape
    assert ts == 1 and zs == 2
    sites, edge = zs * xs * ys, xs * ys
    slices, members = lax.axis_size("ta"), lax.axis_size("gz")
    inner, outer, out, back = routes(slices, members)
    z_inner = [(i, i ^ 1) for i in range(members)]
    z_outer = [(i, (i + 2 * (i % 2) - 1) % members) for i in range(members)]
    t, g = lax.axis_index("ta"), lax.axis_index("gz")
    seam = jnp.logical_or(t % GROUP == GROUP - 1, t % GROUP == 0)
    role = jnp.stack([jnp.logical_and(g % 2 == 1, seam).astype(jnp.int32), g, t % 2, g % 2]).astype(jnp.int32)

    b = source.reshape(sites, d, cols)
    selfs = self_codes.reshape(sites, d, d)
    hops = hop_codes.reshape(sites, d, 4 * d)
    restricts = restrictor.reshape(sites, -1, d)
    field = jax.ShapeDtypeStruct((sites, d, cols), BF16)
    wide = jax.ShapeDtypeStruct((sites, d, cols), F32)
    slab = jax.ShapeDtypeStruct((edge, d, cols), BF16)
    both = ("ta", "gz")

    scales = link_scales.astype(F32).reshape(sites * 5)
    messages = (field, field, slab, slab, field)
    sent = pl.pallas_call(
        hop_terms,
        out_shape=messages,
        in_specs=[SMEM] * 2 + [VMEM] * 2,
        out_specs=(VMEM,) * 5,
        compiler_params=PARAMS,
    )(role, scales, b, hops)
    vector, estimate = b, b
    for sweep in range(ITERS):
        at_relay = lax.ppermute(sent[4], both, out)
        t_outer = lax.ppermute(sent[0], both, outer)
        t_inner = lax.ppermute(sent[1], both, inner)
        from_z_outer = lax.ppermute(sent[2], "gz", z_outer)
        from_z_inner = lax.ppermute(sent[3], "gz", z_inner)
        partial = pl.pallas_call(
            functools.partial(local_terms, (zs, xs, ys, d)),
            out_shape=wide,
            in_specs=[SMEM] + [VMEM] * 5,
            out_specs=VMEM,
            input_output_aliases={1: 0} if sweep else {},
            cost_estimate=LONG,
            compiler_params=PARAMS,
        )(scales, estimate, b, vector, selfs, hops)
        relayed = lax.ppermute(at_relay, both, back)
        partial = pl.pallas_call(
            z_edge_terms,
            out_shape=wide,
            in_specs=[SMEM] * 2 + [VMEM] * 4,
            out_specs=VMEM,
            input_output_aliases={2: 0},
            compiler_params=PARAMS,
        )(role, scales, partial, from_z_inner, from_z_outer, hops)
        came = (partial, t_inner, t_outer, relayed, hops)
        if sweep + 1 < ITERS:
            estimate, vector, *sent = pl.pallas_call(
                sweep_end,
                out_shape=(wide, field) + messages,
                in_specs=[SMEM] * 2 + [VMEM] * 5,
                out_specs=(VMEM,) * 7,
                input_output_aliases={2: 0},
                compiler_params=PARAMS,
            )(role, scales, *came)
    keep = AGG // members
    coarse_d = restricts.shape[1]
    chunk = (keep, coarse_d, cols)
    pair = (2 * keep, coarse_d, cols)
    smoothed, own, away = pl.pallas_call(
        last_end,
        out_shape=(field, jax.ShapeDtypeStruct(pair, F32), jax.ShapeDtypeStruct(pair, BF16)),
        in_specs=[SMEM] * 3 + [VMEM] * 6,
        out_specs=(VMEM,) * 3,
        scratch_shapes=[pltpu.VMEM((AGG, coarse_d, cols), F32)],
        compiler_params=PARAMS,
    )(role, scales, restrict_map, *came, restricts)
    from_core = lax.ppermute(away, "gz", [(i, i ^ 1) for i in range(members)])
    mine, away = pl.pallas_call(
        coarse_step,
        out_shape=(jax.ShapeDtypeStruct(chunk, F32), jax.ShapeDtypeStruct(chunk, BF16)),
        in_specs=[SMEM] + [VMEM] * 2,
        out_specs=(VMEM,) * 2,
        compiler_params=PARAMS,
    )(role, own, from_core)
    from_chip = lax.ppermute(away, "gz", [(i, i ^ 2) for i in range(members)])
    coarse = mine + from_chip.astype(F32)
    return smoothed.reshape(source.shape), coarse.reshape(1, keep, coarse_d, cols)


def solution(mesh):
    site = P("ta", "gz", None, None, None, None)
    return jax.shard_map(
        shards,
        mesh=mesh,
        in_specs=(site, site, site, P("ta", "gz", None, None, None), P("ta", "gz", None, None), site),
        out_specs=(site, P("ta", "gz", None, None)),
        check_vma=False,
    )
```

```python
import functools

import jax
import jax.numpy as jnp
from jax import lax
from jax.experimental import pallas as pl
from jax.experimental.pallas import tpu as pltpu
from jax.sharding import PartitionSpec as P

ITERS = 3
OMEGA = 0.5
AGG = 16
F32 = jnp.float32
BF16 = jnp.bfloat16
VMEM = pl.BlockSpec(memory_space=pltpu.VMEM)
SMEM = pl.BlockSpec(memory_space=pltpu.SMEM)
PARAMS = pltpu.CompilerParams(vmem_limit_bytes=12 * 1024 * 1024)

GROUP = 32
FORWARD_RELAY = {1: 7, 3: 24}
BACKWARD_RELAY = {1: 24, 3: 7}


def routes(slices, members):
    inner, outer, out, back = [], [], [], []
    for t in range(slices):
        for g in range(members):
            here, ahead, behind = (((t + k) % slices) * members + g for k in (0, 1, -1))
            first = t // GROUP * GROUP
            inner.append((here, behind if t % 2 else ahead))
            across = ahead if t % 2 else behind
            relays = {GROUP - 1: FORWARD_RELAY, 0: BACKWARD_RELAY}.get(t % GROUP, {})
            if g in relays:
                relay = (first + relays[g]) * members + g
                out.append((here, relay))
                back.append((relay, across))
            else:
                outer.append((here, across))
    return inner, outer, out, back


def dot(a, b):
    return jnp.dot(a, b, preferred_element_type=F32)


def dot_t(a, b):
    return lax.dot_general(a, b, (((0,), (0,)), ((), ())), preferred_element_type=F32)


def either(parity, first, second):
    for value, pair in enumerate(((first, second), (second, first))):
        yield pl.when(parity == value), *pair


def hop_terms(role, scales, vector, hops, outer, inner, z_outer, z_inner):
    sites, d = vector.shape[:2]
    edge = z_inner.shape[0]
    last = sites - edge
    for when, ahead, behind in either(role[2], inner, outer):

        @when
        def _():
            for s in range(sites):
                ahead[s] = (scales[5 * s + 4] * dot_t(hops[s, :, 3 * d :], vector[s])).astype(BF16)
            behind[...] = vector[...]

    for when, ahead, behind in either(role[3], z_inner, z_outer):

        @when
        def _():
            for s in range(last, sites):
                ahead[s - last] = (scales[5 * s + 3] * dot_t(hops[s, :, 2 * d : 3 * d], vector[s])).astype(BF16)
            behind[...] = vector[:edge]


def local_terms(shape, scales, estimate, source, vector, selfs, hops, partial):
    zs, xs, ys, d = shape

    def at(z, x, y):
        return (z * xs + x % xs) * ys + y % ys

    def fwd(m, s, p):
        return scales[5 * s + m + 1] * dot(hops[s, :, m * d : (m + 1) * d], p)

    def bwd(m, s):
        return scales[5 * s + m + 1] * dot_t(hops[s, :, m * d : (m + 1) * d], vector[s])

    for z in range(zs):
        for x in range(xs):
            for y in range(ys):
                s = at(z, x, y)
                p = vector[s]
                total = p.astype(F32) + scales[5 * s] * dot(selfs[s], p)
                total += fwd(0, s, vector[at(z, x + 1, y)])
                total += fwd(1, s, vector[at(z, x, y + 1)])
                total += bwd(0, at(z, x - 1, y))
                total += bwd(1, at(z, x, y - 1))
                if z + 1 < zs:
                    total += fwd(2, s, vector[at(z + 1, x, y)])
                if z:
                    total += bwd(2, at(z - 1, x, y))
                partial[s] = estimate[s].astype(F32) + OMEGA * (source[s].astype(F32) - total)


def z_edge_terms(role, scales, partial, z_inner, z_outer, hops, done):
    sites, d = partial.shape[:2]
    edge = z_inner.shape[0]
    last = sites - edge
    for when, z_next, z_back in either(role[3], z_inner, z_outer):

        @when
        def _():
            for s in range(edge):
                done[s] = partial[s] - OMEGA * z_back[s].astype(F32)
            for s in range(last, sites):
                term = dot(hops[s, :, 2 * d : 3 * d], z_next[s - last])
                done[s] = partial[s] - OMEGA * scales[5 * s + 3] * term


def new_estimates(role, scales, partial, inner, outer, relayed, hops, store):
    sites, d = partial.shape[:2]
    for when, t_next, t_back in either(role[2], inner, outer):

        @when
        def _():
            for s in range(sites):
                came = [jnp.where(role[0] != 0, relayed[s], ref[s]) if ref is outer else ref[s] for ref in (t_next, t_back)]
                total = scales[5 * s + 4] * dot(hops[s, :, 3 * d :], came[0]) + came[1].astype(F32)
                store(s, partial[s] - OMEGA * total)


def sweep_end(role, scales, partial, inner, outer, relayed, hops, estimate, vector, *messages):
    def store(s, e):
        estimate[s] = e
        vector[s] = e.astype(BF16)

    new_estimates(role, scales, partial, inner, outer, relayed, hops, store)
    hop_terms(role, scales, vector, hops, *messages)


def last_end(role, scales, labels, partial, inner, outer, relayed, hops, restrictor, vector, own, away, sums):
    half = own.shape[0] // 2
    xs, ys = labels.shape[2:]
    sums[...] = jnp.zeros_like(sums)

    def store(s, e):
        vector[s] = e.astype(BF16)

    new_estimates(role, scales, partial, inner, outer, relayed, hops, store)
    for s in range(vector.shape[0]):
        label = labels[0, s // (xs * ys), s // ys % xs, s % ys]
        sums[label] += dot(restrictor[s], vector[s])
    core = role[3]
    for chip in range(2):
        rows = pl.ds(chip * half, half)
        own[rows] = sums[pl.ds((2 * chip + core) * half, half)]
        away[rows] = sums[pl.ds((2 * chip + 1 - core) * half, half)].astype(BF16)


def coarse_step(role, own, came, mine, away):
    half = mine.shape[0]
    chip = role[1] // 2
    here, there = pl.ds(chip * half, half), pl.ds((1 - chip) * half, half)
    mine[...] = own[here] + came[here].astype(F32)
    away[...] = (own[there] + came[there].astype(F32)).astype(BF16)


def shards(source, self_codes, hop_codes, link_scales, restrict_map, restrictor):
    ts, zs, xs, ys, d, cols = source.shape
    assert ts == 1 and zs == 2
    sites, edge = zs * xs * ys, xs * ys
    slices, members = lax.axis_size("ta"), lax.axis_size("gz")
    inner, outer, out, back = routes(slices, members)
    z_inner = [(i, i ^ 1) for i in range(members)]
    z_outer = [(i, (i + 2 * (i % 2) - 1) % members) for i in range(members)]
    t, g = lax.axis_index("ta"), lax.axis_index("gz")
    seam = jnp.logical_or(t % GROUP == GROUP - 1, t % GROUP == 0)
    role = jnp.stack([jnp.logical_and(g % 2 == 1, seam).astype(jnp.int32), g, t % 2, g % 2]).astype(jnp.int32)

    b = source.reshape(sites, d, cols)
    selfs = self_codes.reshape(sites, d, d)
    hops = hop_codes.reshape(sites, d, 4 * d)
    restricts = restrictor.reshape(sites, -1, d)
    field = jax.ShapeDtypeStruct((sites, d, cols), BF16)
    wide = jax.ShapeDtypeStruct((sites, d, cols), F32)
    slab = jax.ShapeDtypeStruct((edge, d, cols), BF16)
    both = ("ta", "gz")

    scales = link_scales.astype(F32).reshape(sites * 5)
    messages = (field, field, slab, slab)
    sent = pl.pallas_call(
        hop_terms,
        out_shape=messages,
        in_specs=[SMEM] * 2 + [VMEM] * 2,
        out_specs=(VMEM,) * 4,
        compiler_params=PARAMS,
    )(role, scales, b, hops)
    vector, estimate = b, b
    for sweep in range(ITERS):
        at_relay = lax.ppermute(sent[0], both, out)
        t_outer = lax.ppermute(sent[0], both, outer)
        t_inner = lax.ppermute(sent[1], both, inner)
        from_z_outer = lax.ppermute(sent[2], "gz", z_outer)
        from_z_inner = lax.ppermute(sent[3], "gz", z_inner)
        partial = pl.pallas_call(
            functools.partial(local_terms, (zs, xs, ys, d)),
            out_shape=wide,
            in_specs=[SMEM] + [VMEM] * 5,
            out_specs=VMEM,
            input_output_aliases={1: 0} if sweep else {},
            compiler_params=PARAMS,
        )(scales, estimate, b, vector, selfs, hops)
        relayed = lax.ppermute(at_relay, both, back)
        partial = pl.pallas_call(
            z_edge_terms,
            out_shape=wide,
            in_specs=[SMEM] * 2 + [VMEM] * 4,
            out_specs=VMEM,
            input_output_aliases={2: 0},
            compiler_params=PARAMS,
        )(role, scales, partial, from_z_inner, from_z_outer, hops)
        came = (partial, t_inner, t_outer, relayed, hops)
        if sweep + 1 < ITERS:
            estimate, vector, *sent = pl.pallas_call(
                sweep_end,
                out_shape=(wide, field) + messages,
                in_specs=[SMEM] * 2 + [VMEM] * 5,
                out_specs=(VMEM,) * 6,
                input_output_aliases={2: 0},
                compiler_params=PARAMS,
            )(role, scales, *came)
    keep = AGG // members
    coarse_d = restricts.shape[1]
    chunk = (keep, coarse_d, cols)
    pair = (2 * keep, coarse_d, cols)
    smoothed, own, away = pl.pallas_call(
        last_end,
        out_shape=(field, jax.ShapeDtypeStruct(pair, F32), jax.ShapeDtypeStruct(pair, BF16)),
        in_specs=[SMEM] * 3 + [VMEM] * 6,
        out_specs=(VMEM,) * 3,
        scratch_shapes=[pltpu.VMEM((AGG, coarse_d, cols), F32)],
        compiler_params=PARAMS,
    )(role, scales, restrict_map, *came, restricts)
    from_core = lax.ppermute(away, "gz", [(i, i ^ 1) for i in range(members)])
    mine, away = pl.pallas_call(
        coarse_step,
        out_shape=(jax.ShapeDtypeStruct(chunk, F32), jax.ShapeDtypeStruct(chunk, BF16)),
        in_specs=[SMEM] + [VMEM] * 2,
        out_specs=(VMEM,) * 2,
        compiler_params=PARAMS,
    )(role, own, from_core)
    from_chip = lax.ppermute(away, "gz", [(i, i ^ 2) for i in range(members)])
    coarse = mine + from_chip.astype(F32)
    return smoothed.reshape(source.shape), coarse.reshape(1, keep, coarse_d, cols)


def solution(mesh):
    site = P("ta", "gz", None, None, None, None)
    return jax.shard_map(
        shards,
        mesh=mesh,
        in_specs=(site, site, site, P("ta", "gz", None, None, None), P("ta", "gz", None, None), site),
        out_specs=(site, P("ta", "gz", None, None)),
        check_vma=False,
    )
```
